32 devices in a mesh: rep: 2 (over y), ep: 4 (over z), tp: 4 (over x, core).
Axes of the slice: x: 2, y: 2, z: 4, core: 2. Of those that a mesh axis runs over, the one named last changes fastest.
Arguments:
- tokens: bfloat16 [256, 4096], P(('rep', 'ep'), 'tp'), parts along dimension 0, may hold values from -200 to 200
- norm_gain: float32 [4096], P('tp'), may hold values from 0.1 to 1.9
- expert_ids: int32 [256, 8], P(('rep', 'ep')), parts along dimension 0, may hold values from 0 to 31, all different within a row; in each aligned block of 32 rows (0 to 31, 32 to 63, ...) at most 16 rows name the same one
- route_weight: float32 [256, 8], P(('rep', 'ep')), parts along dimension 0, may hold values from 0.02 to 0.25
- gate_weight: bfloat16 [32, 4096, 1536], P('ep', None, 'tp'), may hold values from -0.09375 to 0.09375
- up_weight: bfloat16 [32, 4096, 1536], P('ep', None, 'tp'), may hold values from -0.09375 to 0.09375
- down_weight: bfloat16 [32, 1536, 4096], P('ep', 'tp'), may hold values from -0.15625 to 0.15625
Outputs:
- combined: bfloat16 [256, 4096], P(('rep', 'ep'), 'tp'), parts along dimension 0
The draws below stay inside these ranges and needn't reach their ends.
There are 2 independent parts, one for each index of `rep`. The reference program is written for one: setup_inputs(seed, part) draws one part's arguments, and reference() takes and returns one part's arrays. A program takes and returns all parts, laid end to end along the dimension named above; an argument that names none is the same for every part. Nothing has to cross between parts.
Inputs may be any that keep to these rules, and one draw needn't show every extreme that they name: `expert_ids`: in each aligned block of 32 rows (the tokens of one index of ep) no expert is named by more than 16 rows, and in every draw some block names some expert exactly 16 times; a row names 8 different experts.
All inputs are finite; a program needn't handle non-finite values.
Results may differ from the reference program's by a relative error of at most 0.012.
Values may be sent and summed in bfloat16 or wider, within the bound.
A program may use at most 192 MiB of HBM per device.

```python
import math
import jax
import jax.numpy as jnp
import numpy as np
from jax import lax

D = 4096
FFE = 1536
TOP = 8
EXPERTS = 32
TOK_DEV = 32
CAP = 16
TOKENS = 128
N_EP = 4
N_TP = 4


def draw_tokens(key, part):
    key = jax.random.fold_in(key, 11)
    key_base, key_cols, key_rows = jax.random.split(key, 3)
    column = jnp.arange(D, dtype=jnp.float32) / D
    col_scale = jnp.exp(math.log(3.0) * column + math.log(10.0 / 3.0) * jax.random.uniform(key_cols, (D,), jnp.float32))
    base = jnp.clip(jax.random.normal(key_base, (TOKENS, D), jnp.float32), -4.0, 4.0)
    row_scale = jnp.exp(math.log(10.0) * jax.random.uniform(key_rows, (TOKENS, 1), jnp.float32))
    return (base * col_scale * row_scale * 0.25).astype(jnp.bfloat16)


def steps_of(own_key, dims, cuts, low, top_value):
    gain, own = 1.0, jax.random.fold_in(own_key, 6)
    for axis_at, parts in cuts:
        heights = jnp.exp(jax.random.uniform(jax.random.fold_in(own, axis_at), (parts,), jnp.float32, low / len(cuts), top_value / len(cuts)))
        gain = gain * jnp.repeat(heights, dims[axis_at] // parts).reshape([-1 if axis == axis_at else 1 for axis in range(len(dims))])
    return gain


def routed_block(stream_key, own, number, rows, amount, top, bound, lean):
    sequence = jax.random.permutation(stream_key, amount)
    packed, usual = shares(amount, rows * top, bound, lean, True), shares(amount, rows * top, bound, lean, False)
    places = jnp.arange(amount)

    def named(tallies, rotation):
        used = int((tallies > 0).sum())
        fixed = max(1, used // 4)
        moved = fixed + (places - fixed + rotation * (used - fixed)) % max(1, amount - fixed)
        return jnp.zeros((amount,), jnp.int32).at[sequence[jnp.where(places < fixed, places, moved)]].set(jnp.asarray(tallies, jnp.int32))

    tallies = jnp.where(number % 4 == 0, named(packed, number // 4), named(usual, number - number // 4 - 1))
    mixed = jax.random.permutation(jax.random.fold_in(own, 3), amount)
    donor, receiver = mixed[0:amount // 2 * 2:2], mixed[1:amount // 2 * 2:2]
    room = jnp.minimum(tallies[donor] - 1, bound - tallies[receiver]) // 2
    room = jnp.where((donor == sequence[0]) | (receiver == sequence[0]) | (tallies[receiver] == 0), 0, jnp.maximum(room, 0))
    moved = jax.random.randint(jax.random.fold_in(own, 4), (amount // 2,), 0, 1 << 20) % (room + 1)
    tallies = tallies.at[donor].add(-moved).at[receiver].add(moved)
    members = jnp.searchsorted(jnp.cumsum(tallies), jnp.arange(rows * top), side="right").astype(jnp.int32)
    table = members.reshape(top, rows).T
    table = table[jax.random.permutation(jax.random.fold_in(own, 1), rows)]
    rotation = jax.random.randint(jax.random.fold_in(own, 2), (rows, 1), 0, top)
    return jnp.take_along_axis(table, (jnp.arange(top)[None, :] + rotation) % top, axis=1)


def shares(count, total, limit, skew, full):
    portions = [(1 << 20) // math.isqrt(grade ** skew) + 1 for grade in range(1, count + 1)]
    largest = limit if full else min(limit, max(-(-total // count), total * portions[0] // sum(portions)))
    least = 1 if total - largest >= count - 1 else 0
    given, surplus = [largest] + [least] * (count - 1), total - largest - least * (count - 1)
    while surplus > 0:
        movable = [i for i in range(1, count) if given[i] < largest] or [i for i in range(1, count) if given[i] < limit]
        whole, left = sum([portions[i] for i in movable]), surplus
        for i in movable:
            extra = min(limit - given[i], max(1, left * portions[i] // whole), surplus)
            given[i] = given[i] + extra
            surplus = surplus - extra
    return np.array(given)


def bell_draw(stream_key, dims, spread, bound, pieces=(), held_as=jnp.bfloat16):
    array = jax.random.normal(stream_key, dims, jnp.float32) * spread
    if len(pieces) > 0:
        array = steps_of(stream_key, dims, pieces, -0.22, 0.18) * array
    return jnp.clip(array, min=-bound, max=bound).astype(held_as)


def setup_inputs(seed: int = 0, part: int = 0) -> dict:
    streams_of = jax.random.split(jax.random.key(seed), 8)
    own_keys = jax.random.split(jax.random.fold_in(streams_of[7], part), 8)
    tokens = draw_tokens(jax.random.fold_in(jax.random.fold_in(streams_of[7], part), 71), part)
    norm_gain = jnp.clip(1.0 + 0.18 * jax.random.normal(streams_of[1], (D,), jnp.float32), 0.1, 1.9)
    expert_ids_keys = jax.random.split(jax.random.fold_in(own_keys[2], 1), TOKENS // TOK_DEV)
    expert_ids_turns = jax.random.permutation(jax.random.fold_in(own_keys[2], 3), TOKENS // TOK_DEV)
    expert_ids = jax.vmap(lambda own, number: routed_block(jax.random.fold_in(own_keys[2], 2), own, number, TOK_DEV, EXPERTS, TOP, CAP, 2))(expert_ids_keys, expert_ids_turns).reshape((TOKENS, TOP))
    route_weight = jnp.clip(0.02 + 0.23 * jax.random.uniform(own_keys[3], (TOKENS, TOP), jnp.float32) ** steps_of(own_keys[3], (TOKENS, TOP), ((0, 4),), -0.2, 0.2), 0.02, 0.25)
    gate_weight = bell_draw(streams_of[4], (EXPERTS, D, FFE), D ** -0.5, 0.09375, ((0, 4), (2, 4)))
    up_weight = bell_draw(streams_of[5], (EXPERTS, D, FFE), D ** -0.5, 0.09375, ((0, 4), (2, 4)))
    down_weight = bell_draw(streams_of[6], (EXPERTS, FFE, D), FFE ** -0.5, 0.15625, ((0, 4), (1, 4)))
    return dict(tokens=tokens, norm_gain=norm_gain, expert_ids=expert_ids, route_weight=route_weight, gate_weight=gate_weight, up_weight=up_weight, down_weight=down_weight)


def entry_slots(route_ids):
    onehot = (route_ids[..., None] == jnp.arange(EXPERTS, dtype=jnp.int32)).astype(jnp.int32)
    before = jnp.cumsum(onehot, axis=-2) - onehot
    return lax.optimization_barrier(jnp.sum(before * onehot, axis=-1)).astype(jnp.int32)

def reference(tokens, norm_gain, expert_ids, route_weight, gate_weight, up_weight, down_weight):
    wide_tok = tokens.astype(jnp.float32)
    inverse = lax.rsqrt(lax.optimization_barrier(jnp.mean(wide_tok * wide_tok, axis=1, keepdims=True)) + 1e-06)
    normed = (wide_tok * inverse * norm_gain).astype(jnp.bfloat16)
    entries = TOK_DEV * TOP
    blocks = expert_ids.reshape(N_EP, entries)
    slot_ids = entry_slots(blocks)
    source = jnp.arange(N_EP, dtype=jnp.int32)[:, None]
    position = (blocks * (N_EP * CAP) + source * CAP + slot_ids).reshape(-1).astype(jnp.int32)
    token_row = (source * TOK_DEV + jnp.arange(entries, dtype=jnp.int32)[None, :] // TOP).reshape(-1).astype(jnp.int32)
    buffer = jnp.zeros((EXPERTS * N_EP * CAP, D), jnp.bfloat16).at[position].set(normed[token_row])
    buffer = buffer.reshape(EXPERTS, N_EP * CAP, D)
    group_size = FFE // N_TP

    def run_expert(operands):
        row_block, gate_rows, up_rows, down_rows = operands
        gate_act = jnp.dot(row_block, gate_rows, preferred_element_type=jnp.float32)
        up_act = jnp.dot(row_block, up_rows, preferred_element_type=jnp.float32)
        hidden = (jax.nn.silu(gate_act) * up_act).astype(jnp.bfloat16)
        totals = jnp.zeros((row_block.shape[0], D), jnp.float32)
        for group in range(N_TP):
            lower = group * group_size
            partial_value = jnp.dot(hidden[:, lower:lower + group_size], down_rows[lower:lower + group_size, :], preferred_element_type=jnp.float32).astype(jnp.bfloat16)
            partial_value = lax.optimization_barrier(partial_value)
            totals = totals + partial_value.astype(jnp.float32)
        return totals.astype(jnp.bfloat16)
    expert_out = lax.map(run_expert, (buffer, gate_weight, up_weight, down_weight))
    picked = expert_out.reshape(EXPERTS * N_EP * CAP, D)[position].astype(jnp.float32)
    picked = picked.reshape(TOKENS, TOP, D)
    combined = lax.optimization_barrier(jnp.sum(picked * route_weight[:, :, None], axis=1))
    return combined.astype(jnp.bfloat16)
```

```python
import functools

import jax
import jax.numpy as jnp
from jax import lax
from jax.experimental import pallas as pl
from jax.experimental.pallas import tpu as pltpu
from jax.sharding import PartitionSpec as P

LANES = 128
MIB = 1 << 20
SLOTS = 5
MESH = pl.DeviceIdType.MESH


def flip(index, mask):
    bit = 1
    while bit <= mask:
        if mask & bit:
            index = index + bit * (1 - 2 * ((index // bit) % 2))
        bit *= 2
    return index


def kernel(n_ep, n_tp, slots, tok_ref, gain_ref, ids_ref, rw_ref, gate_ref, up_ref, down_ref, out_ref,
           x_all, meta, gu, dn, hid, acc, tx, rx, ztx, zrx, wcol,
           gu_sem, dn_sem, ep_send, ep_recv, tp_send, tp_recv, rs_send, rs_recv, z_send, z_recv):
    me, mt = lax.axis_index("ep"), lax.axis_index("tp")
    rows, width = tok_ref.shape
    local, depth, units = gate_ref.shape
    experts = local * n_ep
    total = rows * n_ep
    bits = n_tp.bit_length() - 1
    wide = units % LANES == 0
    fine = n_ep <= 4
    pieces = n_ep if fine else 1

    def gu_copies(e, slot):
        if wide:
            first, second = gu.at[slot, :, pl.ds(0, units)], gu.at[slot, :, pl.ds(units, units)]
        else:
            first, second = gu.at[slot, 0], gu.at[slot, 1]
        return (
            pltpu.make_async_copy(gate_ref.at[e], first, gu_sem.at[slot, 0]),
            pltpu.make_async_copy(up_ref.at[e], second, gu_sem.at[slot, 1]),
        )

    def dn_copy(d):
        start = pl.multiple_of(flip(mt, d) * width, LANES)
        return pltpu.make_async_copy(down_ref.at[:, :, pl.ds(start, width)], dn.at[d], dn_sem.at[d])

    for e in range(slots):
        for copy in gu_copies(e, e):
            copy.start()
    early = [n_tp - 1, n_tp - 2] if slots < local else list(range(n_tp - 1, -1, -1))
    late = [d for d in range(n_tp - 1, -1, -1) if d not in early]
    for d in early:
        dn_copy(d).start()

    barrier = pltpu.get_barrier_semaphore()

    def greet(t, carry):
        pl.semaphore_signal(barrier, inc=1, device_id={"ep": lax.rem(me + t, n_ep)}, device_id_type=MESH)
        return carry

    lax.fori_loop(1, n_ep, greet, 0)
    for b in range(bits):
        pl.semaphore_signal(barrier, inc=1, device_id={"tp": flip(mt, 1 << b)}, device_id_type=MESH)

    raw = tok_ref[...].astype(jnp.float32)
    x_all[mt, me] = (raw * gain_ref[...]).astype(jnp.bfloat16)
    lane = lax.broadcasted_iota(jnp.int32, (rows, LANES), 1)
    table = jnp.zeros((rows, LANES), jnp.float32)
    for k in range(ids_ref.shape[1]):
        table += jnp.where(ids_ref[:, k:k + 1] == lane, rw_ref[:, k:k + 1], 0.0)
    squares = jnp.sum(raw * raw, axis=1, keepdims=True)
    meta[mt, me] = jnp.where(lane == experts, squares, table)

    pl.semaphore_wait(barrier, n_ep - 1 + bits)

    def ep_copies(t, owner):
        to = {"ep": lax.rem(me + t, n_ep)}
        return [
            pltpu.make_async_remote_copy(
                src_ref=ref.at[mt, owner], dst_ref=ref.at[mt, owner], send_sem=ep_send.at[t, i],
                recv_sem=ep_recv.at[t, i], device_id=to, device_id_type=MESH)
            for i, ref in enumerate((x_all, meta))
        ]

    def tp_copies(p, bit, shard, k):
        to = {"tp": flip(mt, bit)}
        made = []
        for i, ref in enumerate((x_all, meta)):
            view = ref.at[shard, lax.rem(me - p + n_ep, n_ep)] if fine else ref.at[shard]
            made.append(pltpu.make_async_remote_copy(
                src_ref=view, dst_ref=view, send_sem=tp_send.at[p, k, i], recv_sem=tp_recv.at[p, k, i],
                device_id=to, device_id_type=MESH))
        return made

    def ep_start(t, carry):
        for copy in ep_copies(t, me):
            copy.start()
        return carry

    def ep_arrive(t, carry):
        for copy in ep_copies(t, lax.rem(me - t + n_ep, n_ep)):
            copy.wait_recv()
        return carry

    def ep_sent(t, carry):
        for copy in ep_copies(t, me):
            copy.wait_send()
        return carry

    masks = {b: [m for m in range(0, n_tp, 2 << b)] for b in range(bits)}
    lax.fori_loop(1, n_ep, ep_start, 0)
    if not fine:
        lax.fori_loop(1, n_ep, ep_arrive, 0)
    for b in range(bits - 1, -1, -1):
        for p in range(pieces):
            if b == bits - 1:
                if fine and p:
                    ep_arrive(p, 0)
            else:
                for m in masks[b + 1]:
                    k = m | (2 << b)
                    for copy in tp_copies(p, 2 << b, flip(mt, k), k):
                        copy.wait_recv()
            for m in masks[b]:
                for copy in tp_copies(p, 1 << b, flip(mt, m), m | (1 << b)):
                    copy.start()
    for p in range(pieces):
        for m in masks[0]:
            for copy in tp_copies(p, 1, flip(mt, m | 1), m | 1):
                copy.wait_recv()

    heads = meta[mt].reshape(total, LANES)
    sums = meta[0].reshape(total, LANES)
    for j in range(1, n_tp):
        sums = sums + meta[j].reshape(total, LANES)
    lane_all = lax.broadcasted_iota(jnp.int32, (total, LANES), 1)
    mean = jnp.sum(jnp.where(lane_all == experts, sums, 0.0), axis=1, keepdims=True) / depth
    inverse = lax.rsqrt(mean + 1e-6)
    wcol[0] = jnp.broadcast_to(inverse, (total, LANES))
    wcol[1] = heads

    def one_expert(e, slot):
        for copy in gu_copies(e, slot):
            copy.wait()
        x = jnp.concatenate([x_all[j].reshape(total, width) for j in range(n_tp)], axis=1)
        if wide:
            both = jnp.dot(x, gu[slot], preferred_element_type=jnp.float32)
            g, u = both[:, :units], both[:, units:]
        else:
            g = jnp.dot(x, gu[slot, 0], preferred_element_type=jnp.float32)
            u = jnp.dot(x, gu[slot, 1], preferred_element_type=jnp.float32)
        scale = wcol[0][:, 0:1]
        lanes = lax.broadcasted_iota(jnp.int32, (total, LANES), 1)
        share = jnp.sum(jnp.where(lanes == me * local + e, wcol[1], 0.0), axis=1, keepdims=True)
        g, u = g * scale, u * scale
        return (g / (1.0 + jnp.exp(-g)) * u * share).astype(jnp.bfloat16)

    if wide:
        def step(e, carry):
            slot = lax.rem(e, slots)
            hid[:, pl.ds(pl.multiple_of(e * units, LANES), units)] = one_expert(e, slot)
            if slots < local:
                @pl.when(e + slots < local)
                def _():
                    for copy in gu_copies(e + slots, slot):
                        copy.start()

                @pl.when(e == local - slots - 1)
                def _():
                    for d in late:
                        dn_copy(d).start()
            return carry

        lax.fori_loop(0, local, step, 0)
    else:
        for e in range(local):
            hid[:, e * units:(e + 1) * units] = one_expert(e, e)

    def rs_copy(p, d):
        b = (d & -d)
        view = lambda ref: ref.at[d, lax.rem(me + 1 + p, n_ep)] if fine else ref.at[d]
        return pltpu.make_async_remote_copy(
            src_ref=view(tx), dst_ref=view(rx), send_sem=rs_send.at[p, d], recv_sem=rs_recv.at[p, d],
            device_id={"tp": flip(mt, b)}, device_id_type=MESH)

    tile = min(width, 256)

    def z_copy(t, slot):
        return pltpu.make_async_remote_copy(
            src_ref=ztx.at[slot], dst_ref=zrx.at[t], send_sem=z_send.at[t], recv_sem=z_recv.at[t],
            device_id={"ep": lax.rem(me + t, n_ep)}, device_id_type=MESH)

    for d in range(n_tp - 1, -1, -1):
        dn_copy(d).wait()

        def column(n, carry, d=d):
            at = pl.ds(pl.multiple_of(n * tile, LANES), tile)
            weights = dn[d, :, :, at].reshape(local * units, tile)
            value = jnp.dot(hid[...], weights, preferred_element_type=jnp.float32)
            acc[:, :, at] = value.reshape(n_ep, rows, tile)
            return carry

        lax.fori_loop(0, width // tile, column, 0)
        sources = []
        b = 1
        while b < n_tp and not d & b:
            sources.append(d | b)
            b *= 2

        def block(s, sources=sources):
            value = acc[s]
            for source in sources:
                value = value + rx[source, s].astype(jnp.float32)
            return value

        if d:
            for p in range(pieces):
                for source in sources:
                    rs_copy(p, source).wait_recv()
                if fine:
                    s = lax.rem(me + 1 + p, n_ep)
                    tx[d, s] = block(s).astype(jnp.bfloat16)
                else:
                    def fill(s, carry, d=d, block=block):
                        tx[d, s] = block(s).astype(jnp.bfloat16)
                        return carry
                    lax.fori_loop(0, n_ep, fill, 0)
                rs_copy(p, d).start()
        else:
            def arrive(p):
                for source in sources:
                    rs_copy(p, source).wait_recv()

            def send(t, carry):
                s = lax.rem(me + t, n_ep)
                ztx[t] = block(s).astype(jnp.bfloat16)
                z_copy(t, t).start()
                return carry

            if fine:
                for t in range(1, n_ep):
                    arrive(t - 1)
                    send(t, 0)
                arrive(n_ep - 1)
            else:
                arrive(0)
                lax.fori_loop(1, n_ep, send, 0)
            acc[me] = block(me)

    def collect(t, carry):
        z_copy(t, t).wait_recv()
        acc[me] += zrx[t].astype(jnp.float32)
        return carry

    lax.fori_loop(1, n_ep, collect, 0)
    out_ref[...] = acc[me].astype(jnp.bfloat16)

    lax.fori_loop(1, n_ep, ep_sent, 0)
    for p in range(pieces):
        for b in range(bits):
            for m in masks[b]:
                for copy in tp_copies(p, 1 << b, flip(mt, m), m | (1 << b)):
                    copy.wait_send()
        for d in range(1, n_tp):
            rs_copy(p, d).wait_send()

    def z_sent(t, carry):
        z_copy(t, t).wait_send()
        return carry

    lax.fori_loop(1, n_ep, z_sent, 0)


def local_part(n_ep, n_tp, tokens, norm_gain, expert_ids, route_weight, gate_weight, up_weight, down_weight):
    rows, width = tokens.shape
    local, depth, units = gate_weight.shape
    total = rows * n_ep
    wide = units % LANES == 0
    slots = min(local, SLOTS) if wide else local
    pieces = n_ep if n_ep <= 4 else 1
    gu_shape = (slots, depth, 2 * units) if wide else (slots, 2, depth, units)
    vmem = pl.BlockSpec(memory_space=pltpu.VMEM)
    hbm = pl.BlockSpec(memory_space=pl.ANY)
    dma = pltpu.SemaphoreType.DMA
    bf16, f32 = jnp.bfloat16, jnp.float32
    return pl.pallas_call(
        functools.partial(kernel, n_ep, n_tp, slots),
        out_shape=jax.ShapeDtypeStruct((rows, width), bf16),
        in_specs=[vmem] * 4 + [hbm] * 3,
        out_specs=vmem,
        scratch_shapes=[
            pltpu.VMEM((n_tp, n_ep, rows, width), bf16),
            pltpu.VMEM((n_tp, n_ep, rows, LANES), f32),
            pltpu.VMEM(gu_shape, bf16),
            pltpu.VMEM((n_tp, local, units, width), bf16),
            pltpu.VMEM((total, local * units), bf16),
            pltpu.VMEM((n_ep, rows, width), f32),
            pltpu.VMEM((n_tp, n_ep, rows, width), bf16),
            pltpu.VMEM((n_tp, n_ep, rows, width), bf16),
            pltpu.VMEM((n_ep, rows, width), bf16),
            pltpu.VMEM((n_ep, rows, width), bf16),
            pltpu.VMEM((2, total, LANES), f32),
            dma((slots, 2)),
            dma((n_tp,)),
            dma((n_ep, 2)),
            dma((n_ep, 2)),
            dma((pieces, n_tp, 2)),
            dma((pieces, n_tp, 2)),
            dma((pieces, n_tp)),
            dma((pieces, n_tp)),
            dma((n_ep,)),
            dma((n_ep,)),
        ],
        compiler_params=pltpu.CompilerParams(
            collective_id=0, has_side_effects=True, vmem_limit_bytes=62 * MIB
        ),
        cost_estimate=pl.CostEstimate(
            flops=6 * total * local * depth * units,
            bytes_accessed=6 * local * depth * units,
            transcendentals=total * local * units,
        ),
    )(tokens, norm_gain.reshape(1, width), expert_ids, route_weight, gate_weight, up_weight, down_weight)


def solution(mesh):
    in_specs = (
        P(("rep", "ep"), "tp"),
        P("tp"),
        P(("rep", "ep"), None),
        P(("rep", "ep"), None),
        P("ep", None, "tp"),
        P("ep", None, "tp"),
        P("ep", "tp", None),
    )
    run = functools.partial(local_part, mesh.shape["ep"], mesh.shape["tp"])
    return jax.shard_map(
        run, mesh=mesh, in_specs=in_specs, out_specs=P(("rep", "ep"), "tp"), check_vma=False)
```

```python
import functools

import jax
import jax.numpy as jnp
from jax import lax
from jax.experimental import pallas as pl
from jax.experimental.pallas import tpu as pltpu
from jax.sharding import PartitionSpec as P

LANES = 128
MIB = 1 << 20
SLOTS = 5
HALVES = 2
MESH = pl.DeviceIdType.MESH


def flip(index, mask):
    bit = 1
    while bit <= mask:
        if mask & bit:
            index = index + bit * (1 - 2 * ((index // bit) % 2))
        bit *= 2
    return index


def kernel(n_ep, n_tp, slots, tok_ref, gain_ref, ids_ref, rw_ref, gate_ref, up_ref, down_ref, out_ref,
           x_all, meta, gu, dn, hid, acc, tx, rx, ztx, zrx, wcol,
           gu_sem, dn_sem, ep_send, ep_recv, tp_send, tp_recv, rs_send, rs_recv, z_send, z_recv):
    me, mt = lax.axis_index("ep"), lax.axis_index("tp")
    rows, width = tok_ref.shape
    local, depth, units = gate_ref.shape
    experts = local * n_ep
    total = rows * n_ep
    bits = n_tp.bit_length() - 1
    wide = units % LANES == 0
    fine = n_ep <= 4
    pieces = n_ep if fine else 1

    def gu_copies(e, slot):
        if wide:
            first, second = gu.at[slot, :, pl.ds(0, units)], gu.at[slot, :, pl.ds(units, units)]
        else:
            first, second = gu.at[slot, 0], gu.at[slot, 1]
        return (
            pltpu.make_async_copy(gate_ref.at[e], first, gu_sem.at[slot, 0]),
            pltpu.make_async_copy(up_ref.at[e], second, gu_sem.at[slot, 1]),
        )

    def dn_copy(d):
        start = pl.multiple_of(flip(mt, d) * width, LANES)
        return pltpu.make_async_copy(down_ref.at[:, :, pl.ds(start, width)], dn.at[d], dn_sem.at[d])

    for e in range(slots):
        for copy in gu_copies(e, e):
            copy.start()
    early = list(range(n_tp - 1, 0, -1)) if slots < local else list(range(n_tp - 1, -1, -1))
    late = [d for d in range(n_tp - 1, -1, -1) if d not in early]
    for d in early:
        dn_copy(d).start()

    barrier = pltpu.get_barrier_semaphore()

    def greet(t, carry):
        pl.semaphore_signal(barrier, inc=1, device_id={"ep": lax.rem(me + t, n_ep)}, device_id_type=MESH)
        return carry

    lax.fori_loop(1, n_ep, greet, 0)
    for b in range(bits):
        pl.semaphore_signal(barrier, inc=1, device_id={"tp": flip(mt, 1 << b)}, device_id_type=MESH)

    raw = tok_ref[...].astype(jnp.float32)
    x_all[mt, me] = (raw * gain_ref[...]).astype(jnp.bfloat16)
    lane = lax.broadcasted_iota(jnp.int32, (rows, LANES), 1)
    table = jnp.zeros((rows, LANES), jnp.float32)
    for k in range(ids_ref.shape[1]):
        table += jnp.where(ids_ref[:, k:k + 1] == lane, rw_ref[:, k:k + 1], 0.0)
    squares = jnp.sum(raw * raw, axis=1, keepdims=True)
    meta[mt, me] = jnp.where(lane == experts, squares, table)

    pl.semaphore_wait(barrier, n_ep - 1 + bits)

    def ep_copies(t, owner):
        to = {"ep": lax.rem(me + t, n_ep)}
        return [
            pltpu.make_async_remote_copy(
                src_ref=ref.at[mt, owner], dst_ref=ref.at[mt, owner], send_sem=ep_send.at[t, i],
                recv_sem=ep_recv.at[t, i], device_id=to, device_id_type=MESH)
            for i, ref in enumerate((x_all, meta))
        ]

    def tp_copies(p, bit, shard, k):
        to = {"tp": flip(mt, bit)}
        made = []
        for i, ref in enumerate((x_all, meta)):
            view = ref.at[shard, lax.rem(me - p + n_ep, n_ep)] if fine else ref.at[shard]
            made.append(pltpu.make_async_remote_copy(
                src_ref=view, dst_ref=view, send_sem=tp_send.at[p, k, i], recv_sem=tp_recv.at[p, k, i],
                device_id=to, device_id_type=MESH))
        return made

    def ep_start(t, carry):
        for copy in ep_copies(t, me):
            copy.start()
        return carry

    def ep_arrive(t, carry):
        for copy in ep_copies(t, lax.rem(me - t + n_ep, n_ep)):
            copy.wait_recv()
        return carry

    def ep_sent(t, carry):
        for copy in ep_copies(t, me):
            copy.wait_send()
        return carry

    masks = {b: [m for m in range(0, n_tp, 2 << b)] for b in range(bits)}
    lax.fori_loop(1, n_ep, ep_start, 0)
    if not fine:
        lax.fori_loop(1, n_ep, ep_arrive, 0)
    for b in range(bits - 1, -1, -1):
        for p in range(pieces):
            if b == bits - 1:
                if fine and p:
                    ep_arrive(p, 0)
            else:
                for m in masks[b + 1]:
                    k = m | (2 << b)
                    for copy in tp_copies(p, 2 << b, flip(mt, k), k):
                        copy.wait_recv()
            for m in masks[b]:
                for copy in tp_copies(p, 1 << b, flip(mt, m), m | (1 << b)):
                    copy.start()
    for p in range(pieces):
        for m in masks[0]:
            for copy in tp_copies(p, 1, flip(mt, m | 1), m | 1):
                copy.wait_recv()

    heads = meta[mt].reshape(total, LANES)
    sums = meta[0].reshape(total, LANES)
    for j in range(1, n_tp):
        sums = sums + meta[j].reshape(total, LANES)
    lane_all = lax.broadcasted_iota(jnp.int32, (total, LANES), 1)
    mean = jnp.sum(jnp.where(lane_all == experts, sums, 0.0), axis=1, keepdims=True) / depth
    inverse = lax.rsqrt(mean + 1e-6)
    wcol[0] = jnp.broadcast_to(inverse, (total, LANES))
    wcol[1] = heads

    def one_expert(e, slot):
        for copy in gu_copies(e, slot):
            copy.wait()
        x = jnp.concatenate([x_all[j].reshape(total, width) for j in range(n_tp)], axis=1)
        if wide:
            both = jnp.dot(x, gu[slot], preferred_element_type=jnp.float32)
            g, u = both[:, :units], both[:, units:]
        else:
            g = jnp.dot(x, gu[slot, 0], preferred_element_type=jnp.float32)
            u = jnp.dot(x, gu[slot, 1], preferred_element_type=jnp.float32)
        scale = wcol[0][:, 0:1]
        lanes = lax.broadcasted_iota(jnp.int32, (total, LANES), 1)
        share = jnp.sum(jnp.where(lanes == me * local + e, wcol[1], 0.0), axis=1, keepdims=True)
        g, u = g * scale, u * scale
        return (g / (1.0 + jnp.exp(-g)) * u * share).astype(jnp.bfloat16)

    if wide:
        def step(e, carry):
            slot = lax.rem(e, slots)
            hid[:, pl.ds(pl.multiple_of(e * units, LANES), units)] = one_expert(e, slot)
            if slots < local:
                @pl.when(e + slots < local)
                def _():
                    for copy in gu_copies(e + slots, slot):
                        copy.start()

                @pl.when(e == local - slots - 1)
                def _():
                    for d in late:
                        dn_copy(d).start()
            return carry

        lax.fori_loop(0, local, step, 0)
    else:
        for e in range(local):
            hid[:, e * units:(e + 1) * units] = one_expert(e, e)

    half = width // HALVES
    tile = min(half, 256)

    def rs_copy(p, d, h):
        view = lambda ref: ref.at[h, d, lax.rem(me + 1 + p, n_ep)] if fine else ref.at[h, d]
        return pltpu.make_async_remote_copy(
            src_ref=view(tx), dst_ref=view(rx), send_sem=rs_send.at[p, d, h], recv_sem=rs_recv.at[p, d, h],
            device_id={"tp": flip(mt, d & -d)}, device_id_type=MESH)

    def z_copy(t, h):
        return pltpu.make_async_remote_copy(
            src_ref=ztx.at[h, t], dst_ref=zrx.at[h, t], send_sem=z_send.at[t, h], recv_sem=z_recv.at[t, h],
            device_id={"ep": lax.rem(me + t, n_ep)}, device_id_type=MESH)

    def sources_of(d):
        return [d | (1 << b) for b in range(bits) if not d & ((2 << b) - 1)]

    def block(s, d, h):
        value = acc[h if d == 0 else HALVES, s]
        for source in sources_of(d):
            value = value + rx[h, source, s].astype(jnp.float32)
        return value

    def arrive(p, d, h):
        for source in sources_of(d):
            rs_copy(p, source, h).wait_recv()

    def multiply(d, h):
        if h == 0:
            dn_copy(d).wait()
        target = h if d == 0 else HALVES

        def column(n, carry):
            at = pl.ds(pl.multiple_of(n * tile, LANES), tile)
            weights = dn[d, :, :, pl.ds(pl.multiple_of(h * half + n * tile, LANES), tile)]
            value = jnp.dot(hid[...], weights.reshape(local * units, tile), preferred_element_type=jnp.float32)
            acc[target, :, :, at] = value.reshape(n_ep, rows, tile)
            return carry

        lax.fori_loop(0, half // tile, column, 0)

    def pass_on(d, h):
        for p in range(pieces):
            arrive(p, d, h)
            if fine:
                s = lax.rem(me + 1 + p, n_ep)
                tx[h, d, s] = block(s, d, h).astype(jnp.bfloat16)
            else:
                def fill(s, carry):
                    tx[h, d, s] = block(s, d, h).astype(jnp.bfloat16)
                    return carry
                lax.fori_loop(0, n_ep, fill, 0)
            rs_copy(p, d, h).start()

    def finish(h):
        def send(t, carry):
            ztx[h, t] = block(lax.rem(me + t, n_ep), 0, h).astype(jnp.bfloat16)
            z_copy(t, h).start()
            return carry

        if fine:
            for t in range(1, n_ep):
                arrive(t - 1, 0, h)
                send(t, 0)
            arrive(n_ep - 1, 0, h)
        else:
            arrive(0, 0, h)
            lax.fori_loop(1, n_ep, send, 0)
        acc[h, me] = block(me, 0, h)

    for h in range(HALVES):
        for d in range(n_tp - 1, -1, -1):
            multiply(d, h)
            if d:
                pass_on(d, h)
            if h and d == n_tp // 2:
                finish(h - 1)
    finish(HALVES - 1)

    def collect(t, carry):
        for h in range(HALVES):
            z_copy(t, h).wait_recv()
            acc[h, me] += zrx[h, t].astype(jnp.float32)
        return carry

    lax.fori_loop(1, n_ep, collect, 0)
    for h in range(HALVES):
        out_ref[:, h * half:(h + 1) * half] = acc[h, me].astype(jnp.bfloat16)

    lax.fori_loop(1, n_ep, ep_sent, 0)
    for p in range(pieces):
        for b in range(bits):
            for m in masks[b]:
                for copy in tp_copies(p, 1 << b, flip(mt, m), m | (1 << b)):
                    copy.wait_send()
        for d in range(1, n_tp):
            for h in range(HALVES):
                rs_copy(p, d, h).wait_send()

    def z_sent(t, carry):
        for h in range(HALVES):
            z_copy(t, h).wait_send()
        return carry

    lax.fori_loop(1, n_ep, z_sent, 0)


def local_part(n_ep, n_tp, tokens, norm_gain, expert_ids, route_weight, gate_weight, up_weight, down_weight):
    rows, width = tokens.shape
    local, depth, units = gate_weight.shape
    total = rows * n_ep
    wide = units % LANES == 0
    slots = min(local, SLOTS) if wide else local
    pieces = n_ep if n_ep <= 4 else 1
    half = width // HALVES
    gu_shape = (slots, depth, 2 * units) if wide else (slots, 2, depth, units)
    vmem = pl.BlockSpec(memory_space=pltpu.VMEM)
    hbm = pl.BlockSpec(memory_space=pl.ANY)
    dma = pltpu.SemaphoreType.DMA
    bf16, f32 = jnp.bfloat16, jnp.float32
    return pl.pallas_call(
        functools.partial(kernel, n_ep, n_tp, slots),
        out_shape=jax.ShapeDtypeStruct((rows, width), bf16),
        in_specs=[vmem] * 4 + [hbm] * 3,
        out_specs=vmem,
        scratch_shapes=[
            pltpu.VMEM((n_tp, n_ep, rows, width), bf16),
            pltpu.VMEM((n_tp, n_ep, rows, LANES), f32),
            pltpu.VMEM(gu_shape, bf16),
            pltpu.VMEM((n_tp, local, units, width), bf16),
            pltpu.VMEM((total, local * units), bf16),
            pltpu.VMEM((HALVES + 1, n_ep, rows, half), f32),
            pltpu.VMEM((HALVES, n_tp, n_ep, rows, half), bf16),
            pltpu.VMEM((HALVES, n_tp, n_ep, rows, half), bf16),
            pltpu.VMEM((HALVES, n_ep, rows, half), bf16),
            pltpu.VMEM((HALVES, n_ep, rows, half), bf16),
            pltpu.VMEM((2, total, LANES), f32),
            dma((slots, 2)),
            dma((n_tp,)),
            dma((n_ep, 2)),
            dma((n_ep, 2)),
            dma((pieces, n_tp, 2)),
            dma((pieces, n_tp, 2)),
            dma((pieces, n_tp, HALVES)),
            dma((pieces, n_tp, HALVES)),
            dma((n_ep, HALVES)),
            dma((n_ep, HALVES)),
        ],
        compiler_params=pltpu.CompilerParams(
            collective_id=0, has_side_effects=True, vmem_limit_bytes=62 * MIB
        ),
        cost_estimate=pl.CostEstimate(
            flops=6 * total * local * depth * units,
            bytes_accessed=6 * local * depth * units,
            transcendentals=total * local * units,
        ),
    )(tokens, norm_gain.reshape(1, width), expert_ids, route_weight, gate_weight, up_weight, down_weight)


def solution(mesh):
    in_specs = (
        P(("rep", "ep"), "tp"),
        P("tp"),
        P(("rep", "ep"), None),
        P(("rep", "ep"), None),
        P("ep", None, "tp"),
        P("ep", None, "tp"),
        P("ep", "tp", None),
    )
    run = functools.partial(local_part, mesh.shape["ep"], mesh.shape["tp"])
    return jax.shard_map(
        run, mesh=mesh, in_specs=in_specs, out_specs=P(("rep", "ep"), "tp"), check_vma=False)
```
